1024 devices in a mesh: dp: 128 (over x_lo, z, core), mp: 8 (over y, x_hi).
Axes of the slice: x: 4 (x_hi: 2, x_lo: 2; x = x_hi * 2 + x_lo), y: 4, z: 32, core: 2. Of those that a mesh axis runs over, the one named last changes fastest.
Arguments:
- queries: bfloat16 [65536, 3072], P('dp', 'mp'), may hold values from -25 to 25
- keys: bfloat16 [65536, 3072], P('dp', 'mp'), may hold values from -8 to 8
- values: bfloat16 [65536, 3072], P('dp', 'mp'), may hold values from -6 to 6
- grad_out: bfloat16 [65536, 3072], P('dp', 'mp'), may hold values from -0.375 to 0.375
- out_weight: bfloat16 [3072, 3072], P('dp', 'mp'), may hold values from -1.75 to 1.75
Outputs:
- d_queries: bfloat16 [65536, 3072], P('dp', 'mp')
- d_keys: bfloat16 [65536, 3072], P('dp', 'mp')
- d_values: bfloat16 [65536, 3072], P('dp', 'mp')
The draws below stay inside these ranges and needn't reach their ends.
All inputs are finite; a program needn't handle non-finite values.
Results may differ from the reference program's by a relative error of at most 0.0075.
Values may be sent and summed in bfloat16 or wider, within the bound.
No kernel may reach another device: no remote copies, remote signals or barrier semaphores. Data moves between devices by JAX's collectives and lax.ppermute only.
A program may use at most 32 MiB of HBM per device.

```python
import math
import jax
import jax.numpy as jnp
from jax import lax

D = 3072
HEADS = 24
HEAD_SIZE = 128
PATCHES = 256
TOKENS = 65536
HD = 3072


def draw_queries(key, part):
    key = jax.random.fold_in(key, 11)
    first = jax.random.fold_in(key, 0)
    base = jnp.clip(1.4 * jax.random.normal(first, (TOKENS, HD), jnp.float32), -8.0, 8.0)
    return base.astype(jnp.bfloat16)


def draw_keys(key, part):
    key = jax.random.fold_in(key, 12)
    base = jnp.clip(1.4 * jax.random.normal(key, (TOKENS, HD), jnp.float32), -8.0, 8.0)
    return base.astype(jnp.bfloat16)


def block_levels(stream_key, dims, pieces, low, high):
    def one(dim, parts):
        steps = jax.random.uniform(jax.random.fold_in(jax.random.fold_in(stream_key, 6), dim), (parts,), jnp.float32, low / len(pieces), high / len(pieces))
        return jnp.repeat(jnp.exp(steps), dims[dim] // parts).reshape((-1,) + (1,) * (len(dims) - dim - 1))

    gain = one(*pieces[0])
    for cut in pieces[1:]:
        gain = gain * one(*cut)
    return gain


def centred(own_key, dims, scale, bound, cuts=(), dtype=jnp.bfloat16):
    loudness = block_levels(own_key, dims, cuts, -0.22, 0.18) if cuts else 1.0
    result = jax.random.normal(own_key, dims, jnp.float32) * scale * loudness
    return jnp.minimum(jnp.maximum(result, -bound), bound).astype(dtype)


def setup_inputs(seed: int = 0) -> dict:
    arg_keys = jax.random.split(jax.random.key(seed), 6)
    return {
        "queries": draw_queries(jax.random.fold_in(arg_keys[5], 71), 0),
        "keys": draw_keys(jax.random.fold_in(arg_keys[5], 71), 0),
        "values": centred(arg_keys[2], (TOKENS, HD), 1.0, 6.0, ((0, 128), (1, 8))),
        "grad_out": centred(arg_keys[3], (TOKENS, D), 0.0625, 0.375, ((0, 128), (1, 8))),
        "out_weight": centred(arg_keys[4], (D, HD), (max(D // 256, 1)) ** -0.5, 1.75, ((0, 128), (1, 8))),
    }


def reference(queries, keys, values, grad_out, out_weight):
    images = TOKENS // PATCHES
    score_scale = 1.0 / math.sqrt(HEAD_SIZE)

    def split_heads(array):
        return array.reshape(images, PATCHES, HEADS, HEAD_SIZE)

    def softmax_probs(query_img, key_img):
        scores = jnp.einsum('qhd,khd->hqk', query_img.astype(jnp.float32), key_img.astype(jnp.float32)) * score_scale
        return jax.nn.softmax(scores, axis=-1)
    grad_attended = jnp.dot(grad_out, out_weight, preferred_element_type=jnp.float32).astype(jnp.bfloat16)

    def backward_image(block):
        query_img, key_img, value_img, grad_img = block
        probs = softmax_probs(query_img, key_img)
        probs_half = probs.astype(jnp.bfloat16)
        grad_f = grad_img.astype(jnp.float32)
        d_values = jnp.einsum('hqk,qhd->khd', probs_half.astype(jnp.float32), grad_f).astype(jnp.bfloat16)
        d_probs = jnp.einsum('qhd,khd->hqk', grad_f, value_img.astype(jnp.float32))
        row_dot = lax.optimization_barrier(jnp.sum(probs * d_probs, axis=-1, keepdims=True))
        d_scores = (probs * (d_probs - row_dot)).astype(jnp.bfloat16).astype(jnp.float32)
        d_queries = (jnp.einsum('hqk,khd->qhd', d_scores, key_img.astype(jnp.float32)) * score_scale).astype(jnp.bfloat16)
        d_keys = (jnp.einsum('hqk,qhd->khd', d_scores, query_img.astype(jnp.float32)) * score_scale).astype(jnp.bfloat16)
        return (d_queries, d_keys, d_values)
    d_queries, d_keys, d_values = lax.map(backward_image, (split_heads(queries), split_heads(keys), split_heads(values), split_heads(grad_attended)))
    return (d_queries.reshape(TOKENS, HD), d_keys.reshape(TOKENS, HD), d_values.reshape(TOKENS, HD))
```

```python
import math

import jax
import jax.numpy as jnp
from jax import lax
from jax.sharding import PartitionSpec as P

HEAD_SIZE = 128
PATCHES = 256
XLO, Z, CORES = 2, 32, 2
STRIDE = 4
FAR = Z // STRIDE


def dp_index(x, z, c):
    return (x * Z + z % Z) * CORES + c


def everyone():
    return [(x, z, c) for x in range(XLO) for z in range(Z) for c in range(CORES)]


def far_groups():
    return [
        [dp_index(x, r + STRIDE * k, c) for k in range(FAR)]
        for x in range(XLO)
        for r in range(STRIDE)
        for c in range(CORES)
    ]


def z_shift(array, step):
    pairs = [
        (dp_index(x, z + (step if c == 0 else -step), c), dp_index(x, z, c))
        for x, z, c in everyone()
    ]
    return lax.ppermute(array, "dp", pairs)


def gather_weight(weight):
    rows, width = weight.shape
    here = lax.axis_index("dp")
    core = here % CORES
    z = (here // CORES) % Z
    x = here // (CORES * Z)
    far = lax.all_to_all(
        jnp.broadcast_to(weight[None], (FAR, rows, width)),
        "dp",
        0,
        0,
        tiled=True,
        axis_index_groups=far_groups(),
    )
    sign = 1 - 2 * core
    residue = z % STRIDE
    parts = [(far, residue)]
    for step in (1, -1, 2):
        parts.append((z_shift(far, step), (residue + sign * step) % STRIDE))
    column = jnp.zeros((FAR, STRIDE, rows, width), weight.dtype)
    for part, where in parts:
        column = lax.dynamic_update_slice(column, part[:, None], (0, where, 0, 0))
    swap_x = [(dp_index(a, b, c), dp_index(1 - a, b, c)) for a, b, c in everyone()]
    other = lax.ppermute(column, "dp", swap_x)
    both = jnp.where(x == 0, jnp.stack([column, other]), jnp.stack([other, column]))
    swap_c = [(dp_index(a, b, c), dp_index(a, b, 1 - c)) for a, b, c in everyone()]
    across = lax.ppermute(both, "dp", swap_c)
    whole = jnp.where(
        core == 0, jnp.stack([both, across], axis=3), jnp.stack([across, both], axis=3)
    )
    return whole.reshape(XLO * Z * CORES * rows, width)


def body(queries, keys, values, grad_out, out_weight):
    tok_rows = queries.shape[0]
    images = tok_rows // PATCHES
    heads_here = queries.shape[1] // HEAD_SIZE
    width_here = queries.shape[1]
    score_scale = 1.0 / math.sqrt(HEAD_SIZE)

    def split_heads(array):
        return array.reshape(images, PATCHES, heads_here, HEAD_SIZE)

    pieces = 8
    blocks = lax.all_to_all(
        jnp.broadcast_to(grad_out[None], (pieces, tok_rows, width_here)), "mp", 0, 0, tiled=True
    )
    full_weight = gather_weight(out_weight)
    grad_total = jnp.einsum(
        "jtk,jkn->tn",
        blocks,
        full_weight.reshape(pieces, width_here, width_here),
        preferred_element_type=jnp.float32,
    )
    query_img = split_heads(queries)
    key_img = split_heads(keys)
    value_img = split_heads(values)
    scores = (
        jnp.einsum("iqhd,ikhd->ihqk", query_img, key_img, preferred_element_type=jnp.float32)
        * score_scale
    )
    probs = jax.nn.softmax(scores, axis=-1)
    probs_half = probs.astype(jnp.bfloat16)
    grad_img = split_heads(grad_total.astype(jnp.bfloat16))
    d_values = jnp.einsum(
        "ihqk,iqhd->ikhd", probs_half, grad_img, preferred_element_type=jnp.float32
    ).astype(jnp.bfloat16)
    d_probs = jnp.einsum("iqhd,ikhd->ihqk", grad_img, value_img, preferred_element_type=jnp.float32)
    row_dot = jnp.sum(probs * d_probs, axis=-1, keepdims=True)
    d_scores = (probs * (d_probs - row_dot)).astype(jnp.bfloat16)
    d_queries = (
        jnp.einsum("ihqk,ikhd->iqhd", d_scores, key_img, preferred_element_type=jnp.float32)
        * score_scale
    ).astype(jnp.bfloat16)
    d_keys = (
        jnp.einsum("ihqk,iqhd->ikhd", d_scores, query_img, preferred_element_type=jnp.float32)
        * score_scale
    ).astype(jnp.bfloat16)
    return (
        d_queries.reshape(tok_rows, width_here),
        d_keys.reshape(tok_rows, width_here),
        d_values.reshape(tok_rows, width_here),
    )


def solution(mesh):
    placed = (P("dp", "mp"), P("dp", "mp"), P("dp", "mp"), P("dp", "mp"), P("dp", "mp"))
    return jax.shard_map(
        body,
        mesh=mesh,
        in_specs=placed,
        out_specs=(P("dp", "mp"), P("dp", "mp"), P("dp", "mp")),
        check_vma=False,
    )
```

```python
import functools
import math

import jax
import jax.numpy as jnp
import numpy as np
from jax import lax
from jax.experimental import pallas as pl
from jax.experimental.pallas import tpu as pltpu
from jax.sharding import PartitionSpec as P

HEAD_SIZE = 128
PATCHES = 256
XLO, Z, CORES = 2, 32, 2
Y, XHI = 4, 2
STRIDE = 4
FAR = Z // STRIDE
HALVES = 2
QUADS = FAR // HALVES
VMEM = pl.BlockSpec(memory_space=pltpu.VMEM)
SMEM = pl.BlockSpec(memory_space=pltpu.SMEM)
NT = (((1,), (1,)), ((), ()))
TN = (((0,), (0,)), ((), ()))


def dp_index(x, z, c):
    return (x * Z + z % Z) * CORES + c


def everyone():
    return [(x, z, c) for x in range(XLO) for z in range(Z) for c in range(CORES)]


def gather_as_all_to_all(array, groups):
    many = jnp.broadcast_to(array[None], (len(groups[0]),) + array.shape)
    return lax.all_to_all(many, "dp", 0, 0, tiled=True, axis_index_groups=groups)


def far_rows(weight):
    groups = [
        [dp_index(x, r + STRIDE * k, c) for k in range(FAR)]
        for x in range(XLO)
        for r in range(STRIDE)
        for c in range(CORES)
    ]
    return gather_as_all_to_all(weight, groups)


def near_rows(far):
    groups = [
        [dp_index(x, STRIDE * k + r, c) for x in range(XLO) for r in range(STRIDE)]
        for k in range(FAR)
        for c in range(CORES)
    ]
    return gather_as_all_to_all(far, groups)


def core_swap(array):
    return lax.ppermute(
        array, "dp", [(dp_index(x, z, c), dp_index(x, z, 1 - c)) for x, z, c in everyone()]
    )


def arrange_columns(width):
    rows = width // (HALVES * STRIDE * CORES)
    order = (
        np.arange(width)
        .reshape(HALVES, STRIDE, CORES, rows)
        .transpose(2, 1, 0, 3)
        .reshape(width)
    )
    return jnp.asarray(np.arange(width)[:, None] == order[None, :], jnp.bfloat16)


def arrange_kernel(grad_ref, order_ref, out_ref):
    out_ref[...] = jnp.dot(
        grad_ref[...], order_ref[...], preferred_element_type=jnp.float32
    ).astype(out_ref.dtype)


def grad_shift(array, dy, dx):
    mp = Y * XHI
    pairs = []
    for d in range(XLO * Z * CORES):
        sign = 1 - 2 * (d % CORES)
        for y in range(Y):
            for h in range(XHI):
                source = ((y + sign * dy) % Y) * XHI + (h + dx) % XHI
                pairs.append((d * mp + source, d * mp + y * XHI + h))
    return lax.ppermute(array, ("dp", "mp"), pairs)


def arrange(grad):
    rows, width = grad.shape
    return pl.pallas_call(
        arrange_kernel,
        out_shape=jax.ShapeDtypeStruct(grad.shape, grad.dtype),
        in_specs=[VMEM, VMEM],
        out_specs=VMEM,
        name="arrange",
        cost_estimate=pl.CostEstimate(
            flops=2 * rows * width * width, bytes_accessed=6 * rows * width, transcendentals=0
        ),
    )(grad, arrange_columns(width))


def gather_both(weight, grad):
    far = far_rows(weight)
    arranged = arrange(grad)
    across = grad_shift(arranged, 0, 1)
    same = [grad_shift(arranged, dy, 0) for dy in (1, -1, 2)]
    far, across, *same = lax.optimization_barrier((far, across, *same))
    mine = near_rows(far)
    shifted = [grad_shift(across, dy, 0) for dy in (1, -1, 2)]
    mine, *shifted = lax.optimization_barrier((mine, *shifted))
    other = core_swap(mine)
    core = lax.axis_index("dp") & 1
    mp = lax.axis_index("mp")
    y, h, sign = mp >> 1, mp & 1, 1 - 2 * core
    places = [
        (((y + sign * dy) & 3) << 1) | side for side in (h, 1 - h) for dy in (0, 1, -1, 2)
    ]
    places = jnp.stack(places + [core]).astype(jnp.int32)
    return mine, other, [arranged, *same, across, *shifted], places


def probs_kernel(images, heads, query_ref, key_ref, probs_ref):
    scale = 1.0 / math.sqrt(HEAD_SIZE)
    for image in range(images):
        rows = pl.ds(image * PATCHES, PATCHES)
        for head in range(heads):
            cols = pl.ds(head * HEAD_SIZE, HEAD_SIZE)
            scores = (
                lax.dot_general(
                    key_ref[rows, cols],
                    query_ref[rows, cols],
                    NT,
                    preferred_element_type=jnp.float32,
                )
                * scale
            )
            exped = jnp.exp(scores - jnp.max(scores, axis=0, keepdims=True))
            probs_ref[image * heads + head] = exped / jnp.sum(exped, axis=0, keepdims=True)


def tail_kernel(
    images, heads, place_ref, mine_ref, across_ref, probs_ref, query_ref, key_ref, value_ref, *rest
):
    blocks, (dq_ref, dk_ref, dv_ref, weight_ref) = rest[: Y * XHI], rest[Y * XHI :]
    scale = 1.0 / math.sqrt(HEAD_SIZE)
    group = mine_ref.shape[3]
    core = place_ref[8]
    for source, c in ((mine_ref, core), (across_ref, 1 - core)):
        for r in range(STRIDE):
            start = pl.multiple_of((c * STRIDE + r) * group, 16)
            for x in range(XLO):
                for q in range(QUADS):
                    weight_ref[x * QUADS + q, pl.ds(start, group), :] = source[x, r, q]
    for image in range(images):
        rows = pl.ds(image * PATCHES, PATCHES)
        total = None
        for p, block in enumerate(blocks):
            product = jnp.dot(
                block[rows, :], weight_ref[place_ref[p]], preferred_element_type=jnp.float32
            )
            total = product if total is None else total + product
        grad_image = total.astype(jnp.bfloat16)
        for head in range(heads):
            cols = pl.ds(head * HEAD_SIZE, HEAD_SIZE)
            grad = grad_image[:, head * HEAD_SIZE : (head + 1) * HEAD_SIZE]
            probs = probs_ref[image * heads + head]
            dv_ref[rows, cols] = jnp.dot(
                probs.astype(jnp.bfloat16), grad, preferred_element_type=jnp.float32
            ).astype(dv_ref.dtype)
            d_probs = lax.dot_general(
                value_ref[rows, cols], grad, NT, preferred_element_type=jnp.float32
            )
            row_dot = jnp.sum(probs * d_probs, axis=0, keepdims=True)
            d_scores = (probs * (d_probs - row_dot)).astype(jnp.bfloat16)
            dk_ref[rows, cols] = (
                jnp.dot(d_scores, query_ref[rows, cols], preferred_element_type=jnp.float32)
                * scale
            ).astype(dk_ref.dtype)
            dq_ref[rows, cols] = (
                lax.dot_general(
                    d_scores, key_ref[rows, cols], TN, preferred_element_type=jnp.float32
                )
                * scale
            ).astype(dq_ref.dtype)


def body(queries, keys, values, grad_out, out_weight):
    tok_rows, width = queries.shape
    images, heads = tok_rows // PATCHES, width // HEAD_SIZE
    mine, other, blocks, places = gather_both(out_weight, grad_out)
    probs = pl.pallas_call(
        functools.partial(probs_kernel, images, heads),
        out_shape=jax.ShapeDtypeStruct((images * heads, PATCHES, PATCHES), jnp.float32),
        in_specs=[VMEM, VMEM],
        out_specs=VMEM,
        name="probs",
        cost_estimate=pl.CostEstimate(
            flops=2 * tok_rows * PATCHES * width,
            bytes_accessed=4 * tok_rows * width + 4 * heads * tok_rows * PATCHES,
            transcendentals=heads * tok_rows * PATCHES,
        ),
        compiler_params=pltpu.CompilerParams(vmem_limit_bytes=16 << 20),
    )(queries, keys)
    pieces = (XLO, STRIDE, QUADS, HALVES * out_weight.shape[0], width)
    like = jax.ShapeDtypeStruct(queries.shape, queries.dtype)
    return pl.pallas_call(
        functools.partial(tail_kernel, images, heads),
        out_shape=(like, like, like),
        in_specs=[SMEM] + [VMEM] * 14,
        out_specs=(VMEM, VMEM, VMEM),
        scratch_shapes=[pltpu.VMEM((XLO * QUADS, width, width), jnp.bfloat16)],
        name="tail",
        cost_estimate=pl.CostEstimate(
            flops=2 * tok_rows * width * (8 * width + 4 * PATCHES),
            bytes_accessed=2 * (15 * tok_rows * width + 8 * width * width),
            transcendentals=0,
        ),
        compiler_params=pltpu.CompilerParams(vmem_limit_bytes=16 << 20),
    )(
        places,
        mine.reshape(pieces),
        other.reshape(pieces),
        probs,
        queries,
        keys,
        values,
        *blocks,
    )


def solution(mesh):
    placed = (P("dp", "mp"), P("dp", "mp"), P("dp", "mp"), P("dp", "mp"), P("dp", "mp"))
    return jax.shard_map(
        body,
        mesh=mesh,
        in_specs=placed,
        out_specs=(P("dp", "mp"), P("dp", "mp"), P("dp", "mp")),
        check_vma=False,
    )
```

```python
import functools
import math

import jax
import jax.numpy as jnp
import numpy as np
from jax import lax
from jax.experimental import pallas as pl
from jax.experimental.pallas import tpu as pltpu
from jax.sharding import PartitionSpec as P

HEAD_SIZE = 128
PATCHES = 256
XLO, Z, CORES = 2, 32, 2
Y, XHI = 4, 2
STRIDE = 4
FAR = Z // STRIDE
HALVES = 2
QUADS = FAR // HALVES
VMEM = pl.BlockSpec(memory_space=pltpu.VMEM)
ANY = pl.BlockSpec(memory_space=pl.ANY)
SMEM = pl.BlockSpec(memory_space=pltpu.SMEM)
NT = (((1,), (1,)), ((), ()))
TN = (((0,), (0,)), ((), ()))


def dp_index(x, z, c):
    return (x * Z + z % Z) * CORES + c


def everyone():
    return [(x, z, c) for x in range(XLO) for z in range(Z) for c in range(CORES)]


def far_rows(weight):
    groups = [
        [dp_index(x, r + STRIDE * k, c) for k in range(FAR)]
        for x in range(XLO)
        for r in range(STRIDE)
        for c in range(CORES)
    ]
    return lax.all_gather(weight, "dp", axis_index_groups=groups)


def z_shift(array, step):
    pairs = [
        (dp_index(x, z + (1 - 2 * c) * step, c), dp_index(x, z, c)) for x, z, c in everyone()
    ]
    return lax.ppermute(array, "dp", pairs)


def x_swap(array):
    return lax.ppermute(
        array, "dp", [(dp_index(x, z, c), dp_index(1 - x, z, c)) for x, z, c in everyone()]
    )


def core_swap(array):
    return lax.ppermute(
        array, "dp", [(dp_index(x, z, c), dp_index(x, z, 1 - c)) for x, z, c in everyone()]
    )


def arrange_columns(width):
    rows = width // (HALVES * STRIDE * CORES)
    order = (
        np.arange(width)
        .reshape(HALVES, STRIDE, CORES, rows)
        .transpose(2, 1, 0, 3)
        .reshape(width)
    )
    return jnp.asarray(np.arange(width)[:, None] == order[None, :], jnp.bfloat16)


def arrange_kernel(grad_ref, order_ref, out_ref, held, sems):
    held[...] = jnp.dot(
        grad_ref[...], order_ref[...], preferred_element_type=jnp.float32
    ).astype(held.dtype)
    copies = [
        pltpu.make_async_copy(held, out_ref.at[p], sems.at[p]) for p in range(out_ref.shape[0])
    ]
    for copy in copies:
        copy.start()
    for copy in copies:
        copy.wait()


def arranged_copies(grad, count):
    rows, width = grad.shape
    return pl.pallas_call(
        arrange_kernel,
        out_shape=jax.ShapeDtypeStruct((count, rows, width), grad.dtype),
        in_specs=[VMEM, VMEM],
        out_specs=ANY,
        scratch_shapes=[
            pltpu.VMEM((rows, width), grad.dtype),
            pltpu.SemaphoreType.DMA((count,)),
        ],
        name="arrange",
        cost_estimate=pl.CostEstimate(
            flops=2 * rows * width * width,
            bytes_accessed=2 * (count + 1) * rows * width,
            transcendentals=0,
        ),
    )(grad, arrange_columns(width))


STEPS = (0, 2, 1, -1)


def gather_both(weight, grad):
    rows, width = weight.shape
    blocks = lax.all_to_all(arranged_copies(grad, Y * XHI), "mp", 0, 0, tiled=True)
    far = far_rows(weight)
    both = jnp.stack([far, x_swap(far)])
    both, blocks = lax.optimization_barrier((both, blocks))
    mine = [z_shift(both, step) if step else both for step in STEPS]
    pieces = mine + [core_swap(piece) for piece in mine]
    pieces = [
        piece.reshape(XLO, QUADS, HALVES * rows, width) for piece in pieces
    ]
    here = lax.axis_index("dp")
    core, z, x = here & 1, (here >> 1) & (Z - 1), here >> 6
    residues = [
        (z + (1 - 2 * c) * step) & (STRIDE - 1) for c in (core, 1 - core) for step in STEPS
    ]
    places = jnp.stack(residues + [core, x]).astype(jnp.int32)
    return places, blocks, pieces


def tail_kernel(images, heads, place_ref, queries, keys, values, blocks, *rest):
    pieces, (dq_ref, dk_ref, dv_ref), scratch = rest[:8], rest[8:11], rest[11:]
    query_ref, key_ref, value_ref, blocks_ref, weight_ref, probs_ref, sems = scratch
    scale = 1.0 / math.sqrt(HEAD_SIZE)
    group = pieces[0].shape[2]
    count = XLO * QUADS
    core, here = place_ref[8], place_ref[9]
    copies = [(queries, query_ref), (keys, key_ref)]
    for p, piece in enumerate(pieces):
        c = core if p < 4 else 1 - core
        start = pl.multiple_of((c * STRIDE + place_ref[p]) * group, 16)
        for away in range(XLO):
            x = here if away == 0 else 1 - here
            there = weight_ref.at[pl.ds(x * QUADS, QUADS), pl.ds(start, group)]
            copies.append((piece.at[away], there))
    copies += [(blocks.at[j], blocks_ref.at[j]) for j in range(count)]
    copies.append((values, value_ref))
    copies = [pltpu.make_async_copy(*pair, sems.at[i]) for i, pair in enumerate(copies)]
    for copy in copies:
        copy.start()
    for copy in copies[:2]:
        copy.wait()
    for image in range(images):
        rows = pl.ds(image * PATCHES, PATCHES)
        for head in range(heads):
            cols = pl.ds(head * HEAD_SIZE, HEAD_SIZE)
            scores = (
                lax.dot_general(
                    key_ref[rows, cols],
                    query_ref[rows, cols],
                    NT,
                    preferred_element_type=jnp.float32,
                )
                * scale
            )
            exped = jnp.exp(scores - jnp.max(scores, axis=0, keepdims=True))
            probs_ref[image * heads + head] = exped / jnp.sum(exped, axis=0, keepdims=True)
    for copy in copies[2:18]:
        copy.wait()
    for image in range(images):
        rows = pl.ds(image * PATCHES, PATCHES)
        total = None
        for j in range(count):
            if image == 0:
                copies[18 + j].wait()
            product = jnp.dot(
                blocks_ref[j, rows, :], weight_ref[j], preferred_element_type=jnp.float32
            )
            total = product if total is None else total + product
        if image == 0:
            copies[-1].wait()
        grad_image = total.astype(jnp.bfloat16)
        for head in range(heads):
            cols = pl.ds(head * HEAD_SIZE, HEAD_SIZE)
            grad = grad_image[:, head * HEAD_SIZE : (head + 1) * HEAD_SIZE]
            probs = probs_ref[image * heads + head]
            dv_ref[rows, cols] = jnp.dot(
                probs.astype(jnp.bfloat16), grad, preferred_element_type=jnp.float32
            ).astype(dv_ref.dtype)
            d_probs = lax.dot_general(
                value_ref[rows, cols], grad, NT, preferred_element_type=jnp.float32
            )
            row_dot = jnp.sum(probs * d_probs, axis=0, keepdims=True)
            d_scores = (probs * (d_probs - row_dot)).astype(jnp.bfloat16)
            dk_ref[rows, cols] = (
                jnp.dot(d_scores, query_ref[rows, cols], preferred_element_type=jnp.float32)
                * scale
            ).astype(dk_ref.dtype)
            dq_ref[rows, cols] = (
                lax.dot_general(
                    d_scores, key_ref[rows, cols], TN, preferred_element_type=jnp.float32
                )
                * scale
            ).astype(dq_ref.dtype)


def body(queries, keys, values, grad_out, out_weight):
    tok_rows, width = queries.shape
    images, heads = tok_rows // PATCHES, width // HEAD_SIZE
    places, blocks, pieces = gather_both(out_weight, grad_out)
    like = jax.ShapeDtypeStruct(queries.shape, queries.dtype)
    return pl.pallas_call(
        functools.partial(tail_kernel, images, heads),
        out_shape=(like, like, like),
        in_specs=[SMEM] + [ANY] * 12,
        out_specs=(VMEM, VMEM, VMEM),
        scratch_shapes=[
            pltpu.VMEM(queries.shape, jnp.bfloat16),
            pltpu.VMEM(queries.shape, jnp.bfloat16),
            pltpu.VMEM(queries.shape, jnp.bfloat16),
            pltpu.VMEM(blocks.shape, jnp.bfloat16),
            pltpu.VMEM((XLO * QUADS, width, width), jnp.bfloat16),
            pltpu.VMEM((images * heads, PATCHES, PATCHES), jnp.float32),
            pltpu.SemaphoreType.DMA((27,)),
        ],
        name="tail",
        cost_estimate=pl.CostEstimate(
            flops=2 * tok_rows * width * (8 * width + 4 * PATCHES),
            bytes_accessed=2 * (15 * tok_rows * width + 8 * width * width),
            transcendentals=0,
        ),
        compiler_params=pltpu.CompilerParams(vmem_limit_bytes=56 << 20),
    )(places, queries, keys, values, blocks, *pieces)


def solution(mesh):
    placed = (P("dp", "mp"), P("dp", "mp"), P("dp", "mp"), P("dp", "mp"), P("dp", "mp"))
    return jax.shard_map(
        body,
        mesh=mesh,
        in_specs=placed,
        out_specs=(P("dp", "mp"), P("dp", "mp"), P("dp", "mp")),
        check_vma=False,
    )
```

```python
import functools
import math

import jax
import jax.numpy as jnp
import numpy as np
from jax import lax
from jax.experimental import pallas as pl
from jax.experimental.pallas import tpu as pltpu
from jax.sharding import PartitionSpec as P

HEAD_SIZE = 128
PATCHES = 256
XLO, Z, CORES = 2, 32, 2
Y, XHI = 4, 2
STRIDE = 4
FAR = Z // STRIDE
HALVES = 2
QUADS = FAR // HALVES
VMEM = pl.BlockSpec(memory_space=pltpu.VMEM)
ANY = pl.BlockSpec(memory_space=pl.ANY)
SMEM = pl.BlockSpec(memory_space=pltpu.SMEM)
NT = (((1,), (1,)), ((), ()))
TN = (((0,), (0,)), ((), ()))


def dp_index(x, z, c):
    return (x * Z + z % Z) * CORES + c


def everyone():
    return [(x, z, c) for x in range(XLO) for z in range(Z) for c in range(CORES)]


def far_rows(weight):
    groups = [
        [dp_index(x, r + STRIDE * k, c) for k in range(FAR)]
        for x in range(XLO)
        for r in range(STRIDE)
        for c in range(CORES)
    ]
    return lax.all_gather(weight, "dp", axis_index_groups=groups)


def z_shift(array, step):
    pairs = [
        (dp_index(x, z + (1 - 2 * c) * step, c), dp_index(x, z, c)) for x, z, c in everyone()
    ]
    return lax.ppermute(array, "dp", pairs)


def x_swap(array):
    return lax.ppermute(
        array, "dp", [(dp_index(x, z, c), dp_index(1 - x, z, c)) for x, z, c in everyone()]
    )


def core_swap(array):
    return lax.ppermute(
        array, "dp", [(dp_index(x, z, c), dp_index(x, z, 1 - c)) for x, z, c in everyone()]
    )


def arrange_columns(width):
    rows = width // (HALVES * STRIDE * CORES)
    order = (
        np.arange(width)
        .reshape(HALVES, STRIDE, CORES, rows)
        .transpose(2, 1, 0, 3)
        .reshape(width)
    )
    return jnp.asarray(np.arange(width)[:, None] == order[None, :], jnp.bfloat16)


def arrange_kernel(grad_ref, order_ref, out_ref, held, sems):
    held[...] = jnp.dot(
        grad_ref[...], order_ref[...], preferred_element_type=jnp.float32
    ).astype(held.dtype)
    copies = [
        pltpu.make_async_copy(held, out_ref.at[p], sems.at[p]) for p in range(out_ref.shape[0])
    ]
    for copy in copies:
        copy.start()
    for copy in copies:
        copy.wait()


def arranged_copies(grad, count):
    rows, width = grad.shape
    return pl.pallas_call(
        arrange_kernel,
        out_shape=jax.ShapeDtypeStruct((count, rows, width), grad.dtype),
        in_specs=[VMEM, VMEM],
        out_specs=ANY,
        scratch_shapes=[
            pltpu.VMEM((rows, width), grad.dtype),
            pltpu.SemaphoreType.DMA((count,)),
        ],
        name="arrange",
        cost_estimate=pl.CostEstimate(
            flops=2 * rows * width * width,
            bytes_accessed=2 * (count + 1) * rows * width,
            transcendentals=0,
        ),
    )(grad, arrange_columns(width))


STEPS = (0, -1, 1, 2)


def gather_both(weight, grad):
    rows, width = weight.shape
    blocks = lax.all_to_all(arranged_copies(grad, Y * XHI), "mp", 0, 0, tiled=True)
    far = far_rows(weight)
    both = jnp.stack([far, x_swap(far)])
    both, blocks = lax.optimization_barrier((both, blocks))
    mine = [z_shift(both, step) if step else both for step in STEPS]
    pieces = mine + [core_swap(piece) for piece in mine]
    pieces = [
        piece.reshape(XLO, QUADS, HALVES * rows, width) for piece in pieces
    ]
    return blocks, pieces


def tail_kernel(images, heads, here_ref, queries, keys, values, blocks, *rest):
    pieces, (dq_ref, dk_ref, dv_ref), scratch = rest[:8], rest[8:11], rest[11:]
    query_ref, key_ref, value_ref, blocks_ref, weight_ref, probs_ref, sems = scratch
    scale = 1.0 / math.sqrt(HEAD_SIZE)
    group = pieces[0].shape[2]
    count = XLO * QUADS
    here = here_ref[0]
    core, z, here_x = here & 1, (here >> 1) & (Z - 1), here >> 6
    copies = [(queries, query_ref), (keys, key_ref)]
    for p, piece in enumerate(pieces):
        c = core if p < 4 else 1 - core
        residue = (z + (1 - 2 * c) * STEPS[p % 4]) & (STRIDE - 1)
        start = pl.multiple_of((c * STRIDE + residue) * group, 16)
        for away in range(XLO):
            x = here_x if away == 0 else 1 - here_x
            there = weight_ref.at[pl.ds(x * QUADS, QUADS), pl.ds(start, group)]
            copies.append((piece.at[away], there))
    copies += [(blocks.at[j], blocks_ref.at[j]) for j in range(count)]
    copies.append((values, value_ref))
    copies = [pltpu.make_async_copy(*pair, sems.at[i]) for i, pair in enumerate(copies)]
    for copy in copies:
        copy.start()
    for copy in copies[:2]:
        copy.wait()
    for image in range(images):
        rows = pl.ds(image * PATCHES, PATCHES)
        for head in range(heads):
            cols = pl.ds(head * HEAD_SIZE, HEAD_SIZE)
            scores = (
                lax.dot_general(
                    key_ref[rows, cols],
                    query_ref[rows, cols],
                    NT,
                    preferred_element_type=jnp.float32,
                )
                * scale
            )
            exped = jnp.exp(scores - jnp.max(scores, axis=0, keepdims=True))
            probs_ref[image * heads + head] = exped / jnp.sum(exped, axis=0, keepdims=True)
    for copy in copies[2:18]:
        copy.wait()
    for image in range(images):
        rows = pl.ds(image * PATCHES, PATCHES)
        total = None
        for j in range(count):
            if image == 0:
                copies[18 + j].wait()
            product = jnp.dot(
                blocks_ref[j, rows, :], weight_ref[j], preferred_element_type=jnp.float32
            )
            total = product if total is None else total + product
        if image == 0:
            copies[-1].wait()
        grad_image = total.astype(jnp.bfloat16)
        for head in range(heads):
            cols = pl.ds(head * HEAD_SIZE, HEAD_SIZE)
            grad = grad_image[:, head * HEAD_SIZE : (head + 1) * HEAD_SIZE]
            probs = probs_ref[image * heads + head]
            dv_ref[rows, cols] = jnp.dot(
                probs.astype(jnp.bfloat16), grad, preferred_element_type=jnp.float32
            ).astype(dv_ref.dtype)
            d_probs = lax.dot_general(
                value_ref[rows, cols], grad, NT, preferred_element_type=jnp.float32
            )
            row_dot = jnp.sum(probs * d_probs, axis=0, keepdims=True)
            d_scores = (probs * (d_probs - row_dot)).astype(jnp.bfloat16)
            dk_ref[rows, cols] = (
                jnp.dot(d_scores, query_ref[rows, cols], preferred_element_type=jnp.float32)
                * scale
            ).astype(dk_ref.dtype)
            dq_ref[rows, cols] = (
                lax.dot_general(
                    d_scores, key_ref[rows, cols], TN, preferred_element_type=jnp.float32
                )
                * scale
            ).astype(dq_ref.dtype)


def body(queries, keys, values, grad_out, out_weight):
    tok_rows, width = queries.shape
    images, heads = tok_rows // PATCHES, width // HEAD_SIZE
    blocks, pieces = gather_both(out_weight, grad_out)
    here = lax.axis_index("dp").astype(jnp.int32).reshape(1)
    like = jax.ShapeDtypeStruct(queries.shape, queries.dtype)
    return pl.pallas_call(
        functools.partial(tail_kernel, images, heads),
        out_shape=(like, like, like),
        in_specs=[SMEM] + [ANY] * 12,
        out_specs=(VMEM, VMEM, VMEM),
        scratch_shapes=[
            pltpu.VMEM(queries.shape, jnp.bfloat16),
            pltpu.VMEM(queries.shape, jnp.bfloat16),
            pltpu.VMEM(queries.shape, jnp.bfloat16),
            pltpu.VMEM(blocks.shape, jnp.bfloat16),
            pltpu.VMEM((XLO * QUADS, width, width), jnp.bfloat16),
            pltpu.VMEM((images * heads, PATCHES, PATCHES), jnp.float32),
            pltpu.SemaphoreType.DMA((27,)),
        ],
        name="tail",
        cost_estimate=pl.CostEstimate(
            flops=2 * tok_rows * width * (8 * width + 4 * PATCHES),
            bytes_accessed=2 * (15 * tok_rows * width + 8 * width * width),
            transcendentals=0,
        ),
        compiler_params=pltpu.CompilerParams(vmem_limit_bytes=56 << 20),
    )(here, queries, keys, values, blocks, *pieces)


def solution(mesh):
    placed = (P("dp", "mp"), P("dp", "mp"), P("dp", "mp"), P("dp", "mp"), P("dp", "mp"))
    return jax.shard_map(
        body,
        mesh=mesh,
        in_specs=placed,
        out_specs=(P("dp", "mp"), P("dp", "mp"), P("dp", "mp")),
        check_vma=False,
    )
```

```python
import functools
import math

import jax
import jax.numpy as jnp
import numpy as np
from jax import lax
from jax.experimental import pallas as pl
from jax.experimental.pallas import tpu as pltpu
from jax.sharding import PartitionSpec as P

HEAD_SIZE = 128
PATCHES = 256
XLO, Z, CORES = 2, 32, 2
Y, XHI = 4, 2
STRIDE = 4
FAR = Z // STRIDE
HALVES = 2
QUADS = FAR // HALVES
VMEM = pl.BlockSpec(memory_space=pltpu.VMEM)
ANY = pl.BlockSpec(memory_space=pl.ANY)
SMEM = pl.BlockSpec(memory_space=pltpu.SMEM)
NT = (((1,), (1,)), ((), ()))
TN = (((0,), (0,)), ((), ()))


def dp_index(x, z, c):
    return (x * Z + z % Z) * CORES + c


def everyone():
    return [(x, z, c) for x in range(XLO) for z in range(Z) for c in range(CORES)]


def far_rows(weight):
    groups = [
        [dp_index(x, r + STRIDE * k, c) for k in range(FAR)]
        for x in range(XLO)
        for r in range(STRIDE)
        for c in range(CORES)
    ]
    return lax.all_gather(weight, "dp", axis_index_groups=groups)


def z_shift(array, step):
    pairs = [
        (dp_index(x, z + (1 - 2 * c) * step, c), dp_index(x, z, c)) for x, z, c in everyone()
    ]
    return lax.ppermute(array, "dp", pairs)


def x_swap(array):
    return lax.ppermute(
        array, "dp", [(dp_index(x, z, c), dp_index(1 - x, z, c)) for x, z, c in everyone()]
    )


def core_swap(array):
    return lax.ppermute(
        array, "dp", [(dp_index(x, z, c), dp_index(x, z, 1 - c)) for x, z, c in everyone()]
    )


def arrange_columns(width):
    rows = width // (HALVES * STRIDE * CORES)
    order = (
        np.arange(width)
        .reshape(HALVES, STRIDE, CORES, rows)
        .transpose(2, 1, 0, 3)
        .reshape(width)
    )
    return jnp.asarray(np.arange(width)[:, None] == order[None, :], jnp.bfloat16)


def arrange_kernel(grad_ref, order_ref, out_ref, held, sems):
    copies = []
    for half in range(2):
        rows = pl.ds(half * PATCHES, PATCHES)
        held[rows, :] = jnp.dot(
            grad_ref[rows, :], order_ref[...], preferred_element_type=jnp.float32
        ).astype(held.dtype)
        for p in range(out_ref.shape[0]):
            copy = pltpu.make_async_copy(held.at[rows], out_ref.at[p, rows], sems.at[half, p])
            copy.start()
            copies.append(copy)
    for copy in copies:
        copy.wait()


def arranged_copies(grad, count):
    rows, width = grad.shape
    return pl.pallas_call(
        arrange_kernel,
        out_shape=jax.ShapeDtypeStruct((count, rows, width), grad.dtype),
        in_specs=[VMEM, VMEM],
        out_specs=ANY,
        scratch_shapes=[
            pltpu.VMEM((rows, width), grad.dtype),
            pltpu.SemaphoreType.DMA((2, count)),
        ],
        name="arrange",
        cost_estimate=pl.CostEstimate(
            flops=2 * rows * width * width,
            bytes_accessed=2 * (count + 1) * rows * width,
            transcendentals=0,
        ),
    )(grad, arrange_columns(width))


STEPS = (0, -1, 1, 2)


def gather_both(weight, grad):
    rows, width = weight.shape
    blocks = lax.all_to_all(arranged_copies(grad, Y * XHI), "mp", 0, 0, tiled=True)
    far = far_rows(weight)
    both = jnp.stack([far, x_swap(far)])
    both, blocks = lax.optimization_barrier((both, blocks))
    mine = [z_shift(both, step) if step else both for step in STEPS]
    pieces = mine + [core_swap(piece) for piece in mine]
    pieces = [
        piece.reshape(XLO, QUADS, HALVES * rows, width) for piece in pieces
    ]
    return blocks, pieces


def tail_kernel(images, heads, here_ref, queries, keys, values, blocks, *rest):
    pieces, outs, scratch = rest[:8], rest[8:11], rest[11:]
    query_ref, key_ref, value_ref, blocks_ref, weight_ref, probs_ref = scratch[:6]
    dq_ref, dk_ref, dv_ref, sems, out_sems = scratch[6:]
    scale = 1.0 / math.sqrt(HEAD_SIZE)
    group = pieces[0].shape[2]
    count = XLO * QUADS
    here = here_ref[0]
    core, z, here_x = here & 1, (here >> 1) & (Z - 1), here >> 6
    copies = [(queries, query_ref), (keys, key_ref)]
    for p, piece in enumerate(pieces):
        c = core if p < 4 else 1 - core
        residue = (z + (1 - 2 * c) * STEPS[p % 4]) & (STRIDE - 1)
        start = pl.multiple_of((c * STRIDE + residue) * group, 16)
        for away in range(XLO):
            x = here_x if away == 0 else 1 - here_x
            there = weight_ref.at[pl.ds(x * QUADS, QUADS), pl.ds(start, group)]
            copies.append((piece.at[away], there))
    copies += [(blocks.at[j], blocks_ref.at[j]) for j in range(count)]
    copies.append((values, value_ref))
    copies = [pltpu.make_async_copy(*pair, sems.at[i]) for i, pair in enumerate(copies)]
    for copy in copies:
        copy.start()
    for copy in copies[:2]:
        copy.wait()
    for image in range(images):
        rows = pl.ds(image * PATCHES, PATCHES)
        for head in range(heads):
            cols = pl.ds(head * HEAD_SIZE, HEAD_SIZE)
            scores = (
                lax.dot_general(
                    key_ref[rows, cols],
                    query_ref[rows, cols],
                    NT,
                    preferred_element_type=jnp.float32,
                )
                * scale
            )
            exped = jnp.exp(scores - jnp.max(scores, axis=0, keepdims=True))
            probs_ref[image * heads + head] = exped / jnp.sum(exped, axis=0, keepdims=True)
    for copy in copies[2:18]:
        copy.wait()
    writes = []
    for image in range(images):
        rows = pl.ds(image * PATCHES, PATCHES)
        total = None
        for j in range(count):
            if image == 0:
                copies[18 + j].wait()
            product = jnp.dot(
                blocks_ref[j, rows, :], weight_ref[j], preferred_element_type=jnp.float32
            )
            total = product if total is None else total + product
        if image == 0:
            copies[-1].wait()
        grad_image = total.astype(jnp.bfloat16)
        for head in range(heads):
            cols = pl.ds(head * HEAD_SIZE, HEAD_SIZE)
            grad = grad_image[:, head * HEAD_SIZE : (head + 1) * HEAD_SIZE]
            probs = probs_ref[image * heads + head]
            dv_ref[rows, cols] = jnp.dot(
                probs.astype(jnp.bfloat16), grad, preferred_element_type=jnp.float32
            ).astype(dv_ref.dtype)
            d_probs = lax.dot_general(
                value_ref[rows, cols], grad, NT, preferred_element_type=jnp.float32
            )
            row_dot = jnp.sum(probs * d_probs, axis=0, keepdims=True)
            d_scores = (probs * (d_probs - row_dot)).astype(jnp.bfloat16)
            dk_ref[rows, cols] = (
                jnp.dot(d_scores, query_ref[rows, cols], preferred_element_type=jnp.float32)
                * scale
            ).astype(dk_ref.dtype)
            dq_ref[rows, cols] = (
                lax.dot_general(
                    d_scores, key_ref[rows, cols], TN, preferred_element_type=jnp.float32
                )
                * scale
            ).astype(dq_ref.dtype)
        for i, stage in enumerate((dq_ref, dk_ref, dv_ref)):
            write = pltpu.make_async_copy(
                stage.at[rows], outs[i].at[rows], out_sems.at[image, i]
            )
            write.start()
            writes.append(write)
    for write in writes:
        write.wait()


def body(queries, keys, values, grad_out, out_weight):
    tok_rows, width = queries.shape
    images, heads = tok_rows // PATCHES, width // HEAD_SIZE
    blocks, pieces = gather_both(out_weight, grad_out)
    here = lax.axis_index("dp").astype(jnp.int32).reshape(1)
    like = jax.ShapeDtypeStruct(queries.shape, queries.dtype)
    return pl.pallas_call(
        functools.partial(tail_kernel, images, heads),
        out_shape=(like, like, like),
        in_specs=[SMEM] + [ANY] * 12,
        out_specs=(ANY, ANY, ANY),
        scratch_shapes=[
            pltpu.VMEM(queries.shape, jnp.bfloat16),
            pltpu.VMEM(queries.shape, jnp.bfloat16),
            pltpu.VMEM(queries.shape, jnp.bfloat16),
            pltpu.VMEM(blocks.shape, jnp.bfloat16),
            pltpu.VMEM((XLO * QUADS, width, width), jnp.bfloat16),
            pltpu.VMEM((images * heads, PATCHES, PATCHES), jnp.float32),
            pltpu.VMEM(queries.shape, jnp.bfloat16),
            pltpu.VMEM(queries.shape, jnp.bfloat16),
            pltpu.VMEM(queries.shape, jnp.bfloat16),
            pltpu.SemaphoreType.DMA((27,)),
            pltpu.SemaphoreType.DMA((images, 3)),
        ],
        name="tail",
        cost_estimate=pl.CostEstimate(
            flops=2 * tok_rows * width * (8 * width + 4 * PATCHES),
            bytes_accessed=2 * (15 * tok_rows * width + 8 * width * width),
            transcendentals=0,
        ),
        compiler_params=pltpu.CompilerParams(vmem_limit_bytes=56 << 20),
    )(here, queries, keys, values, blocks, *pieces)


def solution(mesh):
    placed = (P("dp", "mp"), P("dp", "mp"), P("dp", "mp"), P("dp", "mp"), P("dp", "mp"))
    return jax.shard_map(
        body,
        mesh=mesh,
        in_specs=placed,
        out_specs=(P("dp", "mp"), P("dp", "mp"), P("dp", "mp")),
        check_vma=False,
    )
```

```python
import functools
import math

import jax
import jax.numpy as jnp
import numpy as np
from jax import lax
from jax.experimental import pallas as pl
from jax.experimental.pallas import tpu as pltpu
from jax.sharding import PartitionSpec as P

HEAD_SIZE = 128
PATCHES = 256
XLO, Z, CORES = 2, 32, 2
Y, XHI = 4, 2
STRIDE = 4
FAR = Z // STRIDE
HALVES = 2
QUADS = FAR // HALVES
VMEM = pl.BlockSpec(memory_space=pltpu.VMEM)
ANY = pl.BlockSpec(memory_space=pl.ANY)
SMEM = pl.BlockSpec(memory_space=pltpu.SMEM)
NT = (((1,), (1,)), ((), ()))
TN = (((0,), (0,)), ((), ()))


def dp_index(x, z, c):
    return (x * Z + z % Z) * CORES + c


def everyone():
    return [(x, z, c) for x in range(XLO) for z in range(Z) for c in range(CORES)]


def far_rows(weight):
    groups = [
        [dp_index(x, r + STRIDE * k, c) for k in range(FAR)]
        for x in range(XLO)
        for r in range(STRIDE)
        for c in range(CORES)
    ]
    return lax.all_gather(weight, "dp", axis_index_groups=groups)


def z_shift(array, step):
    pairs = [
        (dp_index(x, z + (1 - 2 * c) * step, c), dp_index(x, z, c)) for x, z, c in everyone()
    ]
    return lax.ppermute(array, "dp", pairs)


def x_swap(array):
    return lax.ppermute(
        array, "dp", [(dp_index(x, z, c), dp_index(1 - x, z, c)) for x, z, c in everyone()]
    )


def core_swap(array):
    return lax.ppermute(
        array, "dp", [(dp_index(x, z, c), dp_index(x, z, 1 - c)) for x, z, c in everyone()]
    )


def arrange_columns(width):
    rows = width // (HALVES * STRIDE * CORES)
    order = (
        np.arange(width)
        .reshape(HALVES, STRIDE, CORES, rows)
        .transpose(2, 1, 0, 3)
        .reshape(width)
    )
    return jnp.asarray(np.arange(width)[:, None] == order[None, :], jnp.bfloat16)


def arrange_kernel(grad_ref, order_ref, out_ref, held, sems):
    held[...] = jnp.dot(
        grad_ref[...], order_ref[...], preferred_element_type=jnp.float32
    ).astype(held.dtype)
    copies = [
        pltpu.make_async_copy(held, out_ref.at[p], sems.at[p]) for p in range(out_ref.shape[0])
    ]
    for copy in copies:
        copy.start()
    for copy in copies:
        copy.wait()


def arranged_copies(grad, count):
    rows, width = grad.shape
    return pl.pallas_call(
        arrange_kernel,
        out_shape=jax.ShapeDtypeStruct((count, rows, width), grad.dtype),
        in_specs=[VMEM, VMEM],
        out_specs=ANY,
        scratch_shapes=[
            pltpu.VMEM((rows, width), grad.dtype),
            pltpu.SemaphoreType.DMA((count,)),
        ],
        name="arrange",
        cost_estimate=pl.CostEstimate(
            flops=2 * rows * width * width,
            bytes_accessed=2 * (count + 1) * rows * width,
            transcendentals=0,
        ),
    )(grad, arrange_columns(width))


STEPS = (0, -1, 1, 2)


def gather_both(weight, grad):
    rows, width = weight.shape
    blocks = lax.all_to_all(arranged_copies(grad, Y * XHI), "mp", 0, 0, tiled=True)
    far = far_rows(weight)
    both = jnp.stack([far, x_swap(far)])
    both, blocks = lax.optimization_barrier((both, blocks))
    mine = [z_shift(both, step) if step else both for step in STEPS]
    pieces = mine + [core_swap(piece) for piece in mine]
    pieces = [
        piece.reshape(XLO, QUADS, HALVES * rows, width) for piece in pieces
    ]
    return blocks, pieces


def tail_kernel(images, heads, here_ref, queries, keys, values, blocks, *rest):
    pieces, (dq_ref, dk_ref, dv_ref), scratch = rest[:8], rest[8:11], rest[11:]
    query_ref, key_ref, value_ref, blocks_ref, weight_ref, probs_ref, sems = scratch
    scale = 1.0 / math.sqrt(HEAD_SIZE)
    group = pieces[0].shape[2]
    count = XLO * QUADS
    here = here_ref[0]
    core, z, here_x = here & 1, (here >> 1) & (Z - 1), here >> 6
    copies = [(queries, query_ref), (keys, key_ref)]
    for p, piece in enumerate(pieces):
        c = core if p < 4 else 1 - core
        residue = (z + (1 - 2 * c) * STEPS[p % 4]) & (STRIDE - 1)
        start = pl.multiple_of((c * STRIDE + residue) * group, 16)
        for away in range(XLO):
            x = here_x if away == 0 else 1 - here_x
            there = weight_ref.at[pl.ds(x * QUADS, QUADS), pl.ds(start, group)]
            copies.append((piece.at[away], there))
    copies += [(blocks.at[j], blocks_ref.at[j]) for j in range(count)]
    copies.append((values, value_ref))
    copies = [pltpu.make_async_copy(*pair, sems.at[i]) for i, pair in enumerate(copies)]
    for copy in copies:
        copy.start()
    for copy in copies[:2]:
        copy.wait()
    for image in range(images):
        rows = pl.ds(image * PATCHES, PATCHES)
        for head in range(heads):
            cols = pl.ds(head * HEAD_SIZE, HEAD_SIZE)
            scores = (
                lax.dot_general(
                    key_ref[rows, cols],
                    query_ref[rows, cols],
                    NT,
                    preferred_element_type=jnp.float32,
                )
                * scale
            )
            exped = jnp.exp(scores - jnp.max(scores, axis=0, keepdims=True))
            probs_ref[image * heads + head] = exped / jnp.sum(exped, axis=0, keepdims=True)
    for copy in copies[2:18]:
        copy.wait()
    for image in range(images):
        rows = pl.ds(image * PATCHES, PATCHES)
        if image == 0:
            for copy in copies[18:-1]:
                copy.wait()
        total = jnp.dot(
            jnp.concatenate([blocks_ref[j, rows, :] for j in range(count)], axis=1),
            weight_ref[...].reshape(count * weight_ref.shape[1], weight_ref.shape[2]),
            preferred_element_type=jnp.float32,
        )
        if image == 0:
            copies[-1].wait()
        grad_image = total.astype(jnp.bfloat16)
        for head in range(heads):
            cols = pl.ds(head * HEAD_SIZE, HEAD_SIZE)
            grad = grad_image[:, head * HEAD_SIZE : (head + 1) * HEAD_SIZE]
            probs = probs_ref[image * heads + head]
            dv_ref[rows, cols] = jnp.dot(
                probs.astype(jnp.bfloat16), grad, preferred_element_type=jnp.float32
            ).astype(dv_ref.dtype)
            d_probs = lax.dot_general(
                value_ref[rows, cols], grad, NT, preferred_element_type=jnp.float32
            )
            row_dot = jnp.sum(probs * d_probs, axis=0, keepdims=True)
            d_scores = (probs * (d_probs - row_dot)).astype(jnp.bfloat16)
            dk_ref[rows, cols] = (
                jnp.dot(d_scores, query_ref[rows, cols], preferred_element_type=jnp.float32)
                * scale
            ).astype(dk_ref.dtype)
            dq_ref[rows, cols] = (
                lax.dot_general(
                    d_scores, key_ref[rows, cols], TN, preferred_element_type=jnp.float32
                )
                * scale
            ).astype(dq_ref.dtype)


def body(queries, keys, values, grad_out, out_weight):
    tok_rows, width = queries.shape
    images, heads = tok_rows // PATCHES, width // HEAD_SIZE
    blocks, pieces = gather_both(out_weight, grad_out)
    here = lax.axis_index("dp").astype(jnp.int32).reshape(1)
    like = jax.ShapeDtypeStruct(queries.shape, queries.dtype)
    return pl.pallas_call(
        functools.partial(tail_kernel, images, heads),
        out_shape=(like, like, like),
        in_specs=[SMEM] + [ANY] * 12,
        out_specs=(VMEM, VMEM, VMEM),
        scratch_shapes=[
            pltpu.VMEM(queries.shape, jnp.bfloat16),
            pltpu.VMEM(queries.shape, jnp.bfloat16),
            pltpu.VMEM(queries.shape, jnp.bfloat16),
            pltpu.VMEM(blocks.shape, jnp.bfloat16),
            pltpu.VMEM((XLO * QUADS, width, width), jnp.bfloat16),
            pltpu.VMEM((images * heads, PATCHES, PATCHES), jnp.float32),
            pltpu.SemaphoreType.DMA((27,)),
        ],
        name="tail",
        cost_estimate=pl.CostEstimate(
            flops=2 * tok_rows * width * (8 * width + 4 * PATCHES),
            bytes_accessed=2 * (15 * tok_rows * width + 8 * width * width),
            transcendentals=0,
        ),
        compiler_params=pltpu.CompilerParams(vmem_limit_bytes=56 << 20),
    )(here, queries, keys, values, blocks, *pieces)


def solution(mesh):
    placed = (P("dp", "mp"), P("dp", "mp"), P("dp", "mp"), P("dp", "mp"), P("dp", "mp"))
    return jax.shard_map(
        body,
        mesh=mesh,
        in_specs=placed,
        out_specs=(P("dp", "mp"), P("dp", "mp"), P("dp", "mp")),
        check_vma=False,
    )
```
